32 devices in a mesh: section: 4 (over x, core), dom: 8 (over z, y).
Axes of the slice: x: 2, y: 2, z: 4, core: 2. Of those that a mesh axis runs over, the one named last changes fastest.
Arguments:
- features: bfloat16 [4, 1024, 512], P(None, 'dom'), may hold values from -6 to 6
- adjacency: bfloat16 [4, 16, 64, 576], P(None, 'dom'), may hold values from -0.25 to 0.25
- boundary: int32 [4, 8, 8], replicated, may hold values from 0 to 1
- layer_counts: int32 [4], P('section'), may hold values from 0 to 2, as said below
- weights: bfloat16 [4, 2, 512, 512], P('section'), may hold values from -0.25 to 0.25
Outputs:
- stashed: bfloat16 [4, 4, 1024, 512], P('section', None, 'dom')
The draws below stay inside these ranges and needn't reach their ends.
Inputs may be any that keep to these rules, and one draw needn't show every extreme that they name: `layer_counts`: the number of layer slots that section uses; some section uses all 2 and some none. `boundary`: a local block index within the sending partition.
All inputs are finite; a program needn't handle non-finite values.
Results may differ from the reference program's by a relative error of at most 0.009.
Values may be sent and summed in bfloat16 or wider, within the bound.
A program may use at most 64 MiB of HBM per device.

```python
import jax
import jax.numpy as jnp
from jax import lax

D = 512
BLOCK = 64
CAP = 2
NB = 2
MICRO = 4
SLOTS = 9
NODES = 1024
ALL_BLOCKS = 16
N_SECTION = 4
N_DOM = 8


def draw_layer_counts(key, part):
    base = jax.random.randint(key, (N_SECTION,), 0, CAP + 1)
    where_full = jax.random.randint(jax.random.fold_in(key, 1), (), 0, N_SECTION)
    offset = jax.random.randint(jax.random.fold_in(key, 2), (), 1, N_SECTION)
    where_empty = (where_full + offset) % N_SECTION
    position = jnp.arange(N_SECTION)
    base = jnp.where(position == where_full, CAP, base)
    base = jnp.where(position == where_empty, 0, base)
    return base.astype(jnp.int32)


def with_ends(array, key, least, largest):
    dims = array.shape
    spot = [jax.random.randint(jax.random.fold_in(key, axis), (), 0, dims[axis]) for axis in range(len(dims))]
    array = array.at[tuple(spot)].set(least)
    longest = dims.index(max(dims))
    spot[longest] = (spot[longest] + 1) % dims[longest]
    return array.at[tuple(spot)].set(largest)


def steps_of(own_key, dims, cuts, smallest, high):
    factor_of = 1.0
    for dim, blocks in cuts:
        heights = jax.random.uniform(jax.random.fold_in(jax.random.fold_in(own_key, 6), dim), (blocks,), jnp.float32, smallest / len(cuts), high / len(cuts))
        factor_of = factor_of * jnp.repeat(jnp.exp(heights), dims[dim] // blocks).reshape((-1,) + (1,) * (len(dims) - 1 - dim))
    return factor_of


def centred(key, dims, scale, most, pieces=(), kind=jnp.bfloat16):
    loudness = steps_of(key, dims, pieces, -0.22, 0.18) if pieces else 1.0
    result = jax.random.normal(key, dims, jnp.float32) * scale * loudness
    return jnp.minimum(jnp.maximum(result, -most), most).astype(kind)


def setup_inputs(seed: int = 0) -> dict:
    key_list = jax.random.split(jax.random.key(seed), 6)
    return {
        "features": centred(key_list[0], (MICRO, NODES, D), 1.0, 6.0, ((1, 8),)),
        "adjacency": centred(key_list[1], (MICRO, ALL_BLOCKS, BLOCK, SLOTS * BLOCK), (SLOTS * BLOCK) ** -0.5, 0.25, ((1, 8),)),
        "boundary": with_ends(jax.random.randint(key_list[2], (MICRO, N_DOM, N_DOM), 0, NB), jax.random.fold_in(key_list[2], 1), 0, NB - 1).astype(jnp.int32),
        "layer_counts": draw_layer_counts(jax.random.fold_in(key_list[5], 71), 0),
        "weights": centred(key_list[4], (N_SECTION, CAP, D, D), D ** -0.5, 0.25, ((0, 4),)),
    }


def apply_layer(hidden, adj_tiles, bound_ids, weight):
    blocks = hidden.reshape(N_DOM, NB, BLOCK, D)
    senders = jnp.arange(N_DOM, dtype=jnp.int32)
    outbound = blocks[senders[:, None], bound_ids]
    source_part = (senders[:, None] + 1 + jnp.arange(N_DOM - 1, dtype=jnp.int32)[None, :]) % N_DOM
    incoming = outbound[source_part, senders[:, None]]
    sources = jnp.concatenate([blocks, incoming], axis=1).reshape(N_DOM, SLOTS * BLOCK, D)
    tiles = adj_tiles.reshape(N_DOM, NB * BLOCK, SLOTS * BLOCK)
    aggregate = jnp.einsum('pik,pkd->pid', tiles.astype(jnp.float32), sources.astype(jnp.float32))
    aggregate = aggregate.reshape(NODES, D)
    mean_square = lax.optimization_barrier(jnp.mean(aggregate * aggregate, axis=-1, keepdims=True))
    normed = (aggregate * lax.rsqrt(mean_square + 1e-06)).astype(jnp.bfloat16)
    projected = jnp.dot(normed, weight, preferred_element_type=jnp.float32)
    return (hidden.astype(jnp.float32) + jax.nn.relu(projected)).astype(jnp.bfloat16)

def reference(features, adjacency, boundary, layer_counts, weights):
    batched = jax.vmap(apply_layer, in_axes=(0, 0, 0, None))

    def section_step(hidden, inputs):
        section_weights, count = inputs
        for slot in range(CAP):
            updated = batched(hidden, adjacency, boundary, section_weights[slot])
            hidden = jnp.where(slot < count, updated, hidden)
        return (hidden, hidden)
    final_state, stashed = lax.scan(section_step, features, (weights, layer_counts))
    return stashed
```

```python
import functools

import jax
import jax.numpy as jnp
from jax import lax
from jax.experimental import pallas as pl
from jax.experimental.pallas import tpu as pltpu
from jax.sharding import PartitionSpec as P

MESH = pl.DeviceIdType.MESH
ANY = pl.BlockSpec(memory_space=pl.ANY)
SMEM = pl.BlockSpec(memory_space=pltpu.SMEM)
W_PARTS = 2


def part_at(position, n):
    position = lax.rem(position + 2 * n, n)
    return jnp.where(position < n // 2, 2 * position, 2 * (n - position) - 1)


def place_of(part, n):
    return jnp.where(lax.rem(part, 2) == 0, part // 2, n - (part + 1) // 2)


def flip(section, bit):
    core, chip = lax.rem(section, 2), section // 2
    return section + 1 - 2 * core if bit == 0 else section + 2 - 4 * chip


def gather_kernel(n, x_ref, a_ref, w_ref, c_ref, xg, ag, wg, cg,
                  ring_send, ring_recv, w_send, w_recv, c_send, c_recv, own_sem):
    section, part = lax.axis_index("section"), lax.axis_index("dom")
    place = place_of(part, n)
    right, left = part_at(place + 1, n), part_at(place - 1, n)
    core_mate, chip_mate = flip(section, 0), flip(section, 1)
    far_mate = flip(chip_mate, 0)
    slots, depth = w_ref.shape[1], w_ref.shape[2]

    barrier = pltpu.get_barrier_semaphore()
    greeted = [(section, right), (section, left)]
    greeted += [(mate, part) for mate in (core_mate, chip_mate, far_mate)]
    for device in greeted:
        pl.semaphore_signal(barrier, inc=1, device_id=device, device_id_type=MESH)
    pl.semaphore_wait(barrier, len(greeted))

    far, near = n // 2, n - 1 - n // 2
    streams = [
        (0, x_ref, xg, right, -1, far),
        (1, a_ref, ag, left, 1, far),
        (2, x_ref, xg, left, 1, near),
        (3, a_ref, ag, right, -1, near),
    ]

    def ring_copy(stream, step):
        index, own, gathered, target, sign, _ = stream
        block = part_at(place + sign * step, n)
        source = own.at[section] if step == 0 else gathered.at[block]
        return pltpu.make_async_remote_copy(
            src_ref=source, dst_ref=gathered.at[block],
            send_sem=ring_send.at[index, step], recv_sem=ring_recv.at[index, step],
            device_id=(section, target), device_id_type=MESH)

    rows = depth // W_PARTS
    pieces = [(slot, pl.ds(half * rows, rows)) for slot in range(slots) for half in range(W_PARTS)]

    def weight_copy(kind, number):
        slot, span = pieces[number]
        owner = chip_mate if kind == 2 else section
        mate = chip_mate if kind == 0 else core_mate
        source = wg.at[owner, slot, span] if kind == 2 else w_ref.at[0, slot, span]
        return pltpu.make_async_remote_copy(
            src_ref=source, dst_ref=wg.at[owner, slot, span],
            send_sem=w_send.at[kind, number], recv_sem=w_recv.at[kind, number],
            device_id=(mate, part), device_id_type=MESH)

    sends = []

    def go(copy):
        copy.start()
        sends.append(copy)

    for stream in streams:
        go(ring_copy(stream, 0))
    for number in range(len(pieces)):
        go(weight_copy(0, number))
        go(weight_copy(1, number))
    counts = []
    for number, mate in enumerate((core_mate, chip_mate, far_mate)):
        counts.append(pltpu.make_async_remote_copy(
            src_ref=c_ref, dst_ref=cg.at[section], send_sem=c_send.at[number],
            recv_sem=c_recv.at[number], device_id=(mate, part), device_id_type=MESH))
        go(counts[-1])
    own = [
        pltpu.make_async_copy(x_ref.at[section], xg.at[part], own_sem.at[0]),
        pltpu.make_async_copy(a_ref.at[section], ag.at[part], own_sem.at[1]),
        pltpu.make_async_copy(w_ref.at[0], wg.at[section], own_sem.at[2]),
        pltpu.make_async_copy(c_ref, cg.at[section], own_sem.at[3]),
    ]
    for copy in own:
        copy.start()

    for step in range(1, max(far, len(pieces)) + 1):
        for stream in streams:
            if step <= stream[5]:
                ring_copy(stream, step - 1).wait_recv()
                if step < stream[5]:
                    go(ring_copy(stream, step))
        if step <= len(pieces):
            weight_copy(0, step - 1).wait_recv()
            go(weight_copy(2, step - 1))
    for number in range(len(pieces)):
        weight_copy(1, number).wait_recv()
        weight_copy(2, number).wait_recv()
    for copy in counts:
        copy.wait_recv()
    for copy in sends:
        copy.wait_send()
    for copy in own:
        copy.wait()


def layers_kernel(n, cg, bounds, xg, ag, wg, out, hidden, dense, tiles, weights, x_sem, w_sem, a_sem):
    section, part = lax.axis_index("section"), lax.axis_index("dom")
    local_rows, width = xg.shape[1], xg.shape[2]
    half = local_rows // 2
    sections, slots = wg.shape[0], wg.shape[1]
    rows_all = n * local_rows

    x_copy = pltpu.make_async_copy(xg, hidden.at[0], x_sem)
    w_copy = pltpu.make_async_copy(wg, weights, w_sem)

    def a_copy(p, slot):
        return pltpu.make_async_copy(ag.at[p], tiles.at[slot], a_sem.at[slot])

    a_copy(0, 0).start()
    x_copy.start()
    w_copy.start()

    lanes = lax.broadcasted_iota(jnp.int32, (local_rows, local_rows), 1) // half

    def spread(p, carry):
        slot = lax.rem(p, 2)
        a_copy(p, slot).wait()

        @pl.when(p + 1 < n)
        def _():
            a_copy(p + 1, 1 - slot).start()

        rows = pl.ds(pl.multiple_of(p * local_rows, local_rows), local_rows)
        dense[rows, rows] = tiles[slot, :, :local_rows]
        for j in range(n - 1):
            q = lax.rem(p + 1 + j, n)
            start = local_rows + j * half
            block = tiles[slot, :, start:start + half]
            twice = jnp.concatenate([block, block], axis=1)
            pick = bounds[section, q, p]
            columns = pl.ds(pl.multiple_of(q * local_rows, local_rows), local_rows)
            dense[rows, columns] = jnp.where(lanes == pick, twice, jnp.zeros_like(twice))
        return carry

    lax.fori_loop(0, n, spread, 0)
    x_copy.wait()
    w_copy.wait()

    def layer_rows(start, rows, now, later, s, k):
        span = pl.ds(pl.multiple_of(start, rows), rows)
        source = hidden.at[now].reshape(rows_all, width)
        aggregate = jnp.dot(dense[span, :], source[...], preferred_element_type=jnp.float32)
        mean_square = jnp.mean(aggregate * aggregate, axis=-1, keepdims=True)
        normed = (aggregate * lax.rsqrt(mean_square + 1e-06)).astype(jnp.bfloat16)
        projected = jnp.dot(normed, weights[s, k], preferred_element_type=jnp.float32)
        result = source[span, :].astype(jnp.float32) + jnp.maximum(projected, 0.0)
        hidden.at[later].reshape(rows_all, width)[span, :] = result.astype(jnp.bfloat16)

    chunk = min(512, rows_all)
    total = cg[0]
    for s in range(1, sections):
        total = total + cg[s]
    done = jnp.int32(0)
    for s in range(sections):
        for k in range(slots):
            number = done + k
            now = lax.rem(number, 2)
            active = k < cg[s]
            last = number == total - 1

            @pl.when(active & jnp.logical_not(last))
            def _():
                def body(c, carry):
                    layer_rows(c * chunk, chunk, now, 1 - now, s, k)
                    return carry
                lax.fori_loop(0, rows_all // chunk, body, 0)

            @pl.when(active & last)
            def _():
                layer_rows(part * local_rows, local_rows, now, 1 - now, s, k)

        done = done + cg[s]
        out[s] = hidden[lax.rem(done, 2), part]


def trade_kernel(o_ref, out, send, recv, own_sem):
    section, part = lax.axis_index("section"), lax.axis_index("dom")
    chip_mate, core_mate = flip(section, 1), flip(section, 0)
    mates = (flip(chip_mate, 0), chip_mate, core_mate)
    barrier = pltpu.get_barrier_semaphore()
    for mate in mates:
        pl.semaphore_signal(barrier, inc=1, device_id=(mate, part), device_id_type=MESH)
    own = pltpu.make_async_copy(o_ref.at[section], out.at[section], own_sem)
    own.start()
    pl.semaphore_wait(barrier, len(mates))
    copies = [
        pltpu.make_async_remote_copy(
            src_ref=o_ref.at[mate], dst_ref=out.at[section], send_sem=send.at[i],
            recv_sem=recv.at[i], device_id=(mate, part), device_id_type=MESH)
        for i, mate in enumerate(mates)
    ]
    for copy in copies:
        copy.start()
    for copy in copies:
        copy.wait()
    own.wait()


def local(features, adjacency, boundary, layer_counts, weights):
    n = lax.axis_size("dom")
    sections = lax.axis_size("section")
    micro, local_rows, width = features.shape
    slots = weights.shape[1]
    tile_width = adjacency.shape[3]
    tiles = adjacency.reshape(micro, local_rows, tile_width)
    counts = jnp.broadcast_to(layer_counts.reshape(1, 1), (8, 128))
    pieces = slots * W_PARTS
    bf16 = jnp.bfloat16
    dma = pltpu.SemaphoreType.DMA
    xg, ag, wg, cg = pl.pallas_call(
        functools.partial(gather_kernel, n),
        out_shape=[
            jax.ShapeDtypeStruct((n, local_rows, width), bf16),
            jax.ShapeDtypeStruct((n, local_rows, tile_width), bf16),
            jax.ShapeDtypeStruct((sections,) + weights.shape[1:], bf16),
            jax.ShapeDtypeStruct((sections, 8, 128), jnp.int32),
        ],
        in_specs=[ANY] * 4,
        out_specs=[ANY] * 4,
        scratch_shapes=[
            dma((4, n // 2)), dma((4, n // 2)), dma((3, pieces)), dma((3, pieces)),
            dma((3,)), dma((3,)), dma((4,)),
        ],
        compiler_params=pltpu.CompilerParams(collective_id=0, has_side_effects=True),
        name="gather",
    )(features, tiles, weights, counts)

    rows_all = n * local_rows
    mine = pl.pallas_call(
        functools.partial(layers_kernel, n),
        out_shape=jax.ShapeDtypeStruct((sections, local_rows, width), bf16),
        in_specs=[SMEM, SMEM, ANY, ANY, ANY],
        out_specs=pl.BlockSpec(memory_space=pltpu.VMEM),
        scratch_shapes=[
            pltpu.VMEM((2, n, local_rows, width), bf16),
            pltpu.VMEM((rows_all, rows_all), bf16),
            pltpu.VMEM((2, local_rows, tile_width), bf16),
            pltpu.VMEM((sections,) + weights.shape[1:], bf16),
            dma, dma, dma((2,)),
        ],
        compiler_params=pltpu.CompilerParams(vmem_limit_bytes=60 << 20),
        name="layers",
    )(cg[:, 0, 0], boundary, xg, ag, wg)

    out = pl.pallas_call(
        trade_kernel,
        out_shape=jax.ShapeDtypeStruct((sections, local_rows, width), bf16),
        in_specs=[ANY],
        out_specs=ANY,
        scratch_shapes=[dma((3,)), dma((3,)), dma],
        compiler_params=pltpu.CompilerParams(collective_id=1, has_side_effects=True),
        name="trade",
    )(mine)
    return out[None]


def solution(mesh):
    in_specs = (
        P(None, "dom", None),
        P(None, "dom", None, None),
        P(),
        P("section"),
        P("section", None, None, None),
    )
    out_specs = P("section", None, "dom", None)
    return jax.shard_map(local, mesh=mesh, in_specs=in_specs, out_specs=out_specs, check_vma=False)
```

```python
import functools

import jax
import jax.numpy as jnp
from jax import lax
from jax.experimental import pallas as pl
from jax.experimental.pallas import tpu as pltpu
from jax.sharding import PartitionSpec as P

MESH = pl.DeviceIdType.MESH
ANY = pl.BlockSpec(memory_space=pl.ANY)
SMEM = pl.BlockSpec(memory_space=pltpu.SMEM)
W_PARTS = 2


def part_at(position, n):
    position = lax.rem(position + 2 * n, n)
    return jnp.where(position < n // 2, 2 * position, 2 * (n - position) - 1)


def place_of(part, n):
    return jnp.where(lax.rem(part, 2) == 0, part // 2, n - (part + 1) // 2)


def flip(section, bit):
    core, chip = lax.rem(section, 2), section // 2
    return section + 1 - 2 * core if bit == 0 else section + 2 - 4 * chip


def gather_kernel(n, x_ref, a_ref, w_ref, c_ref, xg, ag, wg, cg,
                  ring_send, ring_recv, w_send, w_recv, c_send, c_recv, own_sem):
    section, part = lax.axis_index("section"), lax.axis_index("dom")
    place = place_of(part, n)
    right, left = part_at(place + 1, n), part_at(place - 1, n)
    core_mate, chip_mate = flip(section, 0), flip(section, 1)
    far_mate = flip(chip_mate, 0)
    slots, depth = w_ref.shape[1], w_ref.shape[2]

    barrier = pltpu.get_barrier_semaphore()
    greeted = [(section, right), (section, left)]
    greeted += [(mate, part) for mate in (core_mate, chip_mate, far_mate)]
    for device in greeted:
        pl.semaphore_signal(barrier, inc=1, device_id=device, device_id_type=MESH)
    pl.semaphore_wait(barrier, len(greeted))

    far, near = n // 2, n - 1 - n // 2
    streams = [
        (0, x_ref, xg, right, -1, far),
        (1, a_ref, ag, left, 1, far),
        (2, x_ref, xg, left, 1, near),
        (3, a_ref, ag, right, -1, near),
    ]

    def ring_copy(stream, step):
        index, own, gathered, target, sign, _ = stream
        block = part_at(place + sign * step, n)
        source = own.at[section] if step == 0 else gathered.at[block]
        return pltpu.make_async_remote_copy(
            src_ref=source, dst_ref=gathered.at[block],
            send_sem=ring_send.at[index, step], recv_sem=ring_recv.at[index, step],
            device_id=(section, target), device_id_type=MESH)

    rows = depth // W_PARTS
    pieces = [(slot, pl.ds(half * rows, rows)) for slot in range(slots) for half in range(W_PARTS)]

    def weight_copy(kind, number):
        slot, span = pieces[number]
        owner = chip_mate if kind == 2 else section
        mate = chip_mate if kind == 0 else core_mate
        source = wg.at[owner, slot, span] if kind == 2 else w_ref.at[0, slot, span]
        return pltpu.make_async_remote_copy(
            src_ref=source, dst_ref=wg.at[owner, slot, span],
            send_sem=w_send.at[kind, number], recv_sem=w_recv.at[kind, number],
            device_id=(mate, part), device_id_type=MESH)

    sends = []

    def go(copy):
        copy.start()
        sends.append(copy)

    for stream in streams:
        go(ring_copy(stream, 0))
    for number in range(len(pieces)):
        go(weight_copy(0, number))
        go(weight_copy(1, number))
    counts = []
    for number, mate in enumerate((core_mate, chip_mate, far_mate)):
        counts.append(pltpu.make_async_remote_copy(
            src_ref=c_ref, dst_ref=cg.at[section], send_sem=c_send.at[number],
            recv_sem=c_recv.at[number], device_id=(mate, part), device_id_type=MESH))
        go(counts[-1])
    own = pltpu.make_async_copy(c_ref, cg.at[section], own_sem)
    own.start()

    for step in range(1, max(far, len(pieces)) + 1):
        for stream in streams:
            if step <= stream[5]:
                ring_copy(stream, step - 1).wait_recv()
                if step < stream[5]:
                    go(ring_copy(stream, step))
        if step <= len(pieces):
            weight_copy(0, step - 1).wait_recv()
            go(weight_copy(2, step - 1))
    for number in range(len(pieces)):
        weight_copy(1, number).wait_recv()
        weight_copy(2, number).wait_recv()
    for copy in counts:
        copy.wait_recv()
    for copy in sends:
        copy.wait_send()
    own.wait()


def layers_kernel(n, cg, bounds, x_ref, a_ref, w_ref, xg, ag, wg, out, hidden, dense, tiles, weights, x_sem, w_sem, a_sem):
    section, part = lax.axis_index("section"), lax.axis_index("dom")
    local_rows, width = xg.shape[1], xg.shape[2]
    half = local_rows // 2
    sections, slots = wg.shape[0], wg.shape[1]
    rows_all = n * local_rows

    def fetch(index, here, own, gathered, target, sem):
        @pl.when(index == here)
        def _():
            pltpu.make_async_copy(own, target, sem).start()

        @pl.when(index != here)
        def _():
            pltpu.make_async_copy(gathered.at[index], target, sem).start()

    def fetch_tiles(p, slot):
        fetch(p, part, a_ref.at[section], ag, tiles.at[slot], a_sem.at[slot])

    def fetch_rows(p, carry):
        fetch(p, part, x_ref.at[section], xg, hidden.at[0, p], x_sem)
        return carry

    fetch_tiles(0, 0)
    lax.fori_loop(0, n, fetch_rows, 0)
    for s in range(sections):
        fetch(s, section, w_ref.at[0], wg, weights.at[s], w_sem)

    lanes = lax.broadcasted_iota(jnp.int32, (local_rows, local_rows), 1) // half

    def spread(p, carry):
        slot = lax.rem(p, 2)
        pltpu.make_async_copy(ag.at[p], tiles.at[slot], a_sem.at[slot]).wait()

        @pl.when(p + 1 < n)
        def _():
            fetch_tiles(p + 1, 1 - slot)

        rows = pl.ds(pl.multiple_of(p * local_rows, local_rows), local_rows)
        dense[rows, rows] = tiles[slot, :, :local_rows]
        for j in range(n - 1):
            q = lax.rem(p + 1 + j, n)
            start = local_rows + j * half
            block = tiles[slot, :, start:start + half]
            twice = jnp.concatenate([block, block], axis=1)
            pick = bounds[section, q, p]
            columns = pl.ds(pl.multiple_of(q * local_rows, local_rows), local_rows)
            dense[rows, columns] = jnp.where(lanes == pick, twice, jnp.zeros_like(twice))
        return carry

    lax.fori_loop(0, n, spread, 0)
    pltpu.make_async_copy(xg, hidden.at[0], x_sem).wait()
    pltpu.make_async_copy(wg, weights, w_sem).wait()

    def layer_rows(start, rows, now, later, s, k):
        span = pl.ds(pl.multiple_of(start, rows), rows)
        source = hidden.at[now].reshape(rows_all, width)
        aggregate = jnp.dot(dense[span, :], source[...], preferred_element_type=jnp.float32)
        mean_square = jnp.mean(aggregate * aggregate, axis=-1, keepdims=True)
        normed = (aggregate * lax.rsqrt(mean_square + 1e-06)).astype(jnp.bfloat16)
        projected = jnp.dot(normed, weights[s, k], preferred_element_type=jnp.float32)
        result = source[span, :].astype(jnp.float32) + jnp.maximum(projected, 0.0)
        hidden.at[later].reshape(rows_all, width)[span, :] = result.astype(jnp.bfloat16)

    chunk = min(512, rows_all)
    counts = [cg[s, 0, 0] for s in range(sections)]
    total = sum(counts)
    done = jnp.int32(0)
    for s in range(sections):
        for k in range(slots):
            number = done + k
            now = lax.rem(number, 2)
            active = k < counts[s]
            last = number == total - 1

            @pl.when(active & jnp.logical_not(last))
            def _():
                def body(c, carry):
                    layer_rows(c * chunk, chunk, now, 1 - now, s, k)
                    return carry
                lax.fori_loop(0, rows_all // chunk, body, 0)

            @pl.when(active & last)
            def _():
                layer_rows(part * local_rows, local_rows, now, 1 - now, s, k)

        done = done + counts[s]
        out[s] = hidden[lax.rem(done, 2), part]


def trade_kernel(o_ref, out, send, recv, own_sem):
    section, part = lax.axis_index("section"), lax.axis_index("dom")
    chip_mate, core_mate = flip(section, 1), flip(section, 0)
    mates = (flip(chip_mate, 0), chip_mate, core_mate)
    barrier = pltpu.get_barrier_semaphore()
    for mate in mates:
        pl.semaphore_signal(barrier, inc=1, device_id=(mate, part), device_id_type=MESH)
    own = pltpu.make_async_copy(o_ref.at[section], out.at[section], own_sem)
    own.start()
    pl.semaphore_wait(barrier, len(mates))
    copies = [
        pltpu.make_async_remote_copy(
            src_ref=o_ref.at[mate], dst_ref=out.at[section], send_sem=send.at[i],
            recv_sem=recv.at[i], device_id=(mate, part), device_id_type=MESH)
        for i, mate in enumerate(mates)
    ]
    for copy in copies:
        copy.start()
    for copy in copies:
        copy.wait()
    own.wait()


def local(features, adjacency, boundary, layer_counts, weights):
    n = lax.axis_size("dom")
    sections = lax.axis_size("section")
    micro, local_rows, width = features.shape
    slots = weights.shape[1]
    tile_width = adjacency.shape[3]
    tiles = adjacency.reshape(micro, local_rows, tile_width)
    counts = jnp.broadcast_to(layer_counts.reshape(1, 1), (8, 128))
    pieces = slots * W_PARTS
    bf16 = jnp.bfloat16
    dma = pltpu.SemaphoreType.DMA
    xg, ag, wg, cg = pl.pallas_call(
        functools.partial(gather_kernel, n),
        out_shape=[
            jax.ShapeDtypeStruct((n, local_rows, width), bf16),
            jax.ShapeDtypeStruct((n, local_rows, tile_width), bf16),
            jax.ShapeDtypeStruct((sections,) + weights.shape[1:], bf16),
            jax.ShapeDtypeStruct((sections, 8, 128), jnp.int32),
        ],
        in_specs=[ANY] * 4,
        out_specs=[ANY] * 4,
        scratch_shapes=[
            dma((4, n // 2)), dma((4, n // 2)), dma((3, pieces)), dma((3, pieces)),
            dma((3,)), dma((3,)), dma,
        ],
        compiler_params=pltpu.CompilerParams(collective_id=0, has_side_effects=True),
        name="gather",
    )(features, tiles, weights, counts)

    rows_all = n * local_rows
    mine = pl.pallas_call(
        functools.partial(layers_kernel, n),
        out_shape=jax.ShapeDtypeStruct((sections, local_rows, width), bf16),
        in_specs=[SMEM, SMEM] + [ANY] * 6,
        out_specs=pl.BlockSpec(memory_space=pltpu.VMEM),
        scratch_shapes=[
            pltpu.VMEM((2, n, local_rows, width), bf16),
            pltpu.VMEM((rows_all, rows_all), bf16),
            pltpu.VMEM((2, local_rows, tile_width), bf16),
            pltpu.VMEM((sections,) + weights.shape[1:], bf16),
            dma, dma, dma((2,)),
        ],
        compiler_params=pltpu.CompilerParams(vmem_limit_bytes=60 << 20),
        name="layers",
    )(cg, boundary, features, tiles, weights, xg, ag, wg)

    out = pl.pallas_call(
        trade_kernel,
        out_shape=jax.ShapeDtypeStruct((sections, local_rows, width), bf16),
        in_specs=[pl.BlockSpec(memory_space=pltpu.VMEM)],
        out_specs=pl.BlockSpec(memory_space=pltpu.VMEM),
        scratch_shapes=[dma((3,)), dma((3,)), dma],
        compiler_params=pltpu.CompilerParams(collective_id=1, has_side_effects=True),
        name="trade",
    )(mine)
    return out[None]


def solution(mesh):
    in_specs = (
        P(None, "dom", None),
        P(None, "dom", None, None),
        P(),
        P("section"),
        P("section", None, None, None),
    )
    out_specs = P("section", None, "dom", None)
    return jax.shard_map(local, mesh=mesh, in_specs=in_specs, out_specs=out_specs, check_vma=False)
```

```python
import functools

import jax
import jax.numpy as jnp
from jax import lax
from jax.experimental import pallas as pl
from jax.experimental.pallas import tpu as pltpu
from jax.sharding import PartitionSpec as P

MESH = pl.DeviceIdType.MESH
ANY = pl.BlockSpec(memory_space=pl.ANY)
SMEM = pl.BlockSpec(memory_space=pltpu.SMEM)
W_PARTS = 2


def part_at(position, n):
    position = lax.rem(position + 2 * n, n)
    return jnp.where(position < n // 2, 2 * position, 2 * (n - position) - 1)


def place_of(part, n):
    return jnp.where(lax.rem(part, 2) == 0, part // 2, n - (part + 1) // 2)


def flip(section, bit):
    core, chip = lax.rem(section, 2), section // 2
    return section + 1 - 2 * core if bit == 0 else section + 2 - 4 * chip


def gather_kernel(n, bounds, x_ref, a_ref, w_ref, c_ref, xg, dg, wg, cg,
                  ag, dense, d_sem, a_sem, ring_send, ring_recv, w_send, w_recv, c_send, c_recv, own_sem):
    section, part = lax.axis_index("section"), lax.axis_index("dom")
    place = place_of(part, n)
    right, left = part_at(place + 1, n), part_at(place - 1, n)
    core_mate, chip_mate = flip(section, 0), flip(section, 1)
    far_mate = flip(chip_mate, 0)
    slots, depth = w_ref.shape[1], w_ref.shape[2]

    tiles_in = pltpu.make_async_copy(a_ref.at[section], ag.at[part], a_sem)
    tiles_in.start()
    barrier = pltpu.get_barrier_semaphore()
    greeted = [(section, right), (section, left)]
    greeted += [(mate, part) for mate in (core_mate, chip_mate, far_mate)]
    for device in greeted:
        pl.semaphore_signal(barrier, inc=1, device_id=device, device_id_type=MESH)
    pl.semaphore_wait(barrier, len(greeted))

    far, near = n // 2, n - 1 - n // 2
    streams = [
        (0, x_ref, xg, right, -1, far),
        (1, a_ref, ag, left, 1, far),
        (2, x_ref, xg, left, 1, near),
        (3, a_ref, ag, right, -1, near),
    ]

    def ring_copy(stream, step):
        index, own, gathered, target, sign, _ = stream
        block = part_at(place + sign * step, n)
        source = own.at[section] if step == 0 else gathered.at[block]
        return pltpu.make_async_remote_copy(
            src_ref=source, dst_ref=gathered.at[block],
            send_sem=ring_send.at[index, step], recv_sem=ring_recv.at[index, step],
            device_id=(section, target), device_id_type=MESH)

    rows = depth // W_PARTS
    pieces = [(slot, pl.ds(half * rows, rows)) for slot in range(slots) for half in range(W_PARTS)]

    def weight_copy(kind, number):
        slot, span = pieces[number]
        owner = chip_mate if kind == 2 else section
        mate = chip_mate if kind == 0 else core_mate
        source = wg.at[owner, slot, span] if kind == 2 else w_ref.at[0, slot, span]
        return pltpu.make_async_remote_copy(
            src_ref=source, dst_ref=wg.at[owner, slot, span],
            send_sem=w_send.at[kind, number], recv_sem=w_recv.at[kind, number],
            device_id=(mate, part), device_id_type=MESH)

    sends = []

    def go(copy):
        copy.start()
        sends.append(copy)

    for stream in streams:
        go(ring_copy(stream, 0))
    for number in range(len(pieces)):
        go(weight_copy(0, number))
        go(weight_copy(1, number))
    counts = []
    for number, mate in enumerate((core_mate, chip_mate, far_mate)):
        counts.append(pltpu.make_async_remote_copy(
            src_ref=c_ref, dst_ref=cg.at[section], send_sem=c_send.at[number],
            recv_sem=c_recv.at[number], device_id=(mate, part), device_id_type=MESH))
        go(counts[-1])
    own = pltpu.make_async_copy(c_ref, cg.at[section], own_sem)
    own.start()
    tiles_in.wait()

    local_rows = ag.shape[1]
    half = local_rows // 2
    lanes = lax.broadcasted_iota(jnp.int32, (local_rows, local_rows), 1) // half

    def spread(number, p):
        rows = pl.ds(pl.multiple_of(p * local_rows, local_rows), local_rows)
        dense[rows, rows] = ag[p, :, :local_rows]

        def put(j, block):
            q = lax.rem(p + 1 + j, n)
            columns = pl.ds(pl.multiple_of(q * local_rows, local_rows), local_rows)
            twice = jnp.concatenate([block, block], axis=1)
            dense[rows, columns] = jnp.where(lanes == bounds[section, q, p], twice, jnp.zeros_like(twice))

        def pair(c, carry):
            both = ag[p, :, pl.ds(pl.multiple_of((c + 1) * local_rows, local_rows), local_rows)]
            put(2 * c, both[:, :half])
            put(2 * c + 1, both[:, half:])
            return carry

        lax.fori_loop(0, (n - 1) // 2, pair, 0)
        put(n - 2, ag[p, :, (n // 2) * local_rows:])
        copy = pltpu.make_async_copy(dense.at[rows], dg.at[rows], d_sem.at[number])
        copy.start()
        return copy

    spreads = [spread(0, part)]

    for step in range(1, max(far, len(pieces)) + 1):
        for stream in streams:
            if step <= stream[5]:
                ring_copy(stream, step - 1).wait_recv()
                if step < stream[5]:
                    go(ring_copy(stream, step))
        if step <= len(pieces):
            weight_copy(0, step - 1).wait_recv()
            go(weight_copy(2, step - 1))
        for stream in (streams[1], streams[3]):
            if step <= stream[5]:
                spreads.append(spread(len(spreads), part_at(place + stream[4] * step, n)))
    for number in range(len(pieces)):
        weight_copy(1, number).wait_recv()
        weight_copy(2, number).wait_recv()
    for copy in counts:
        copy.wait_recv()
    for copy in sends:
        copy.wait_send()
    own.wait()
    for copy in spreads:
        copy.wait()


def layers_kernel(n, cg, x_ref, w_ref, xg, dg, wg, out, hidden, dense, weights, x_sem, d_sem, w_sem):
    section, part = lax.axis_index("section"), lax.axis_index("dom")
    local_rows, width = xg.shape[1], xg.shape[2]
    sections, slots = wg.shape[0], wg.shape[1]
    rows_all = n * local_rows

    def fetch(index, here, own, gathered, target, sem):
        @pl.when(index == here)
        def _():
            pltpu.make_async_copy(own, target, sem).start()

        @pl.when(index != here)
        def _():
            pltpu.make_async_copy(gathered.at[index], target, sem).start()

    def fetch_rows(p, carry):
        fetch(p, part, x_ref.at[section], xg, hidden.at[0, p], x_sem)
        return carry

    d_copy = pltpu.make_async_copy(dg, dense, d_sem)
    d_copy.start()
    lax.fori_loop(0, n, fetch_rows, 0)
    for s in range(sections):
        fetch(s, section, w_ref.at[0], wg, weights.at[s], w_sem.at[s])
    pltpu.make_async_copy(xg, hidden.at[0], x_sem).wait()
    d_copy.wait()

    def layer_rows(start, rows, now, later, s, k):
        span = pl.ds(pl.multiple_of(start, rows), rows)
        source = hidden.at[now].reshape(rows_all, width)
        aggregate = jnp.dot(dense[span, :], source[...], preferred_element_type=jnp.float32)
        mean_square = jnp.mean(aggregate * aggregate, axis=-1, keepdims=True)
        normed = (aggregate * lax.rsqrt(mean_square + 1e-06)).astype(jnp.bfloat16)
        projected = jnp.dot(normed, weights[s, k], preferred_element_type=jnp.float32)
        result = source[span, :].astype(jnp.float32) + jnp.maximum(projected, 0.0)
        hidden.at[later].reshape(rows_all, width)[span, :] = result.astype(jnp.bfloat16)

    chunk = min(512, rows_all)
    counts = [cg[s, 0, 0] for s in range(sections)]
    total = sum(counts)
    done = jnp.int32(0)
    for s in range(sections):
        pltpu.make_async_copy(wg.at[s], weights.at[s], w_sem.at[s]).wait()
        for k in range(slots):
            number = done + k
            now = lax.rem(number, 2)
            active = k < counts[s]
            last = number == total - 1

            @pl.when(active & jnp.logical_not(last))
            def _():
                def body(c, carry):
                    layer_rows(c * chunk, chunk, now, 1 - now, s, k)
                    return carry
                lax.fori_loop(0, rows_all // chunk, body, 0)

            @pl.when(active & last)
            def _():
                layer_rows(part * local_rows, local_rows, now, 1 - now, s, k)

        done = done + counts[s]
        out[s] = hidden[lax.rem(done, 2), part]


def trade_kernel(o_ref, out, send, recv, own_sem):
    section, part = lax.axis_index("section"), lax.axis_index("dom")
    chip_mate, core_mate = flip(section, 1), flip(section, 0)
    mates = (flip(chip_mate, 0), chip_mate, core_mate)
    barrier = pltpu.get_barrier_semaphore()
    for mate in mates:
        pl.semaphore_signal(barrier, inc=1, device_id=(mate, part), device_id_type=MESH)
    own = pltpu.make_async_copy(o_ref.at[section], out.at[section], own_sem)
    own.start()
    pl.semaphore_wait(barrier, len(mates))
    copies = [
        pltpu.make_async_remote_copy(
            src_ref=o_ref.at[mate], dst_ref=out.at[section], send_sem=send.at[i],
            recv_sem=recv.at[i], device_id=(mate, part), device_id_type=MESH)
        for i, mate in enumerate(mates)
    ]
    for copy in copies:
        copy.start()
    for copy in copies:
        copy.wait()
    own.wait()


def local(features, adjacency, boundary, layer_counts, weights):
    n = lax.axis_size("dom")
    sections = lax.axis_size("section")
    micro, local_rows, width = features.shape
    slots = weights.shape[1]
    tile_width = adjacency.shape[3]
    tiles = adjacency.reshape(micro, local_rows, tile_width)
    counts = jnp.broadcast_to(layer_counts.reshape(1, 1), (8, 128))
    pieces = slots * W_PARTS
    bf16 = jnp.bfloat16
    dma = pltpu.SemaphoreType.DMA
    rows_all = n * local_rows
    xg, dg, wg, cg = pl.pallas_call(
        functools.partial(gather_kernel, n),
        out_shape=[
            jax.ShapeDtypeStruct((n, local_rows, width), bf16),
            jax.ShapeDtypeStruct((rows_all, rows_all), bf16),
            jax.ShapeDtypeStruct((sections,) + weights.shape[1:], bf16),
            jax.ShapeDtypeStruct((sections, 8, 128), jnp.int32),
        ],
        in_specs=[SMEM] + [ANY] * 4,
        out_specs=[ANY] * 4,
        scratch_shapes=[
            pltpu.VMEM((n, local_rows, tile_width), bf16),
            pltpu.VMEM((rows_all, rows_all), bf16),
            dma((n,)), dma,
            dma((4, n // 2)), dma((4, n // 2)), dma((3, pieces)), dma((3, pieces)),
            dma((3,)), dma((3,)), dma,
        ],
        compiler_params=pltpu.CompilerParams(
            collective_id=0, has_side_effects=True, vmem_limit_bytes=60 << 20),
        name="gather",
    )(boundary, features, tiles, weights, counts)

    mine = pl.pallas_call(
        functools.partial(layers_kernel, n),
        out_shape=jax.ShapeDtypeStruct((sections, local_rows, width), bf16),
        in_specs=[SMEM] + [ANY] * 5,
        out_specs=pl.BlockSpec(memory_space=pltpu.VMEM),
        scratch_shapes=[
            pltpu.VMEM((2, n, local_rows, width), bf16),
            pltpu.VMEM((rows_all, rows_all), bf16),
            pltpu.VMEM((sections,) + weights.shape[1:], bf16),
            dma, dma, dma((sections,)),
        ],
        compiler_params=pltpu.CompilerParams(vmem_limit_bytes=60 << 20),
        name="layers",
    )(cg, features, weights, xg, dg, wg)

    out = pl.pallas_call(
        trade_kernel,
        out_shape=jax.ShapeDtypeStruct((sections, local_rows, width), bf16),
        in_specs=[pl.BlockSpec(memory_space=pltpu.VMEM)],
        out_specs=pl.BlockSpec(memory_space=pltpu.VMEM),
        scratch_shapes=[dma((3,)), dma((3,)), dma],
        compiler_params=pltpu.CompilerParams(collective_id=1, has_side_effects=True),
        name="trade",
    )(mine)
    return out[None]


def solution(mesh):
    in_specs = (
        P(None, "dom", None),
        P(None, "dom", None, None),
        P(),
        P("section"),
        P("section", None, None, None),
    )
    out_specs = P("section", None, "dom", None)
    return jax.shard_map(local, mesh=mesh, in_specs=in_specs, out_specs=out_specs, check_vma=False)
```

```python
import functools

import jax
import jax.numpy as jnp
from jax import lax
from jax.experimental import pallas as pl
from jax.experimental.pallas import tpu as pltpu
from jax.sharding import PartitionSpec as P

MESH = pl.DeviceIdType.MESH
ANY = pl.BlockSpec(memory_space=pl.ANY)
SMEM = pl.BlockSpec(memory_space=pltpu.SMEM)
W_PARTS = 2


def part_at(position, n):
    position = lax.rem(position + 2 * n, n)
    return jnp.where(position < n // 2, 2 * position, 2 * (n - position) - 1)


def place_of(part, n):
    return jnp.where(lax.rem(part, 2) == 0, part // 2, n - (part + 1) // 2)


def flip(section, bit):
    core, chip = lax.rem(section, 2), section // 2
    return section + 1 - 2 * core if bit == 0 else section + 2 - 4 * chip


def gather_kernel(n, bounds, x_ref, a_ref, w_ref, c_ref, xg, dg, wg, cg,
                  ag, dense, d_sem, a_sem, ring_send, ring_recv, w_send, w_recv, c_send, c_recv, own_sem):
    section, part = lax.axis_index("section"), lax.axis_index("dom")
    place = place_of(part, n)
    right, left = part_at(place + 1, n), part_at(place - 1, n)
    core_mate, chip_mate = flip(section, 0), flip(section, 1)
    far_mate = flip(chip_mate, 0)
    slots, depth = w_ref.shape[1], w_ref.shape[2]

    tiles_in = pltpu.make_async_copy(a_ref.at[section], ag.at[part], a_sem)
    tiles_in.start()
    barrier = pltpu.get_barrier_semaphore()
    greeted = [(section, right), (section, left)]
    greeted += [(mate, part) for mate in (core_mate, chip_mate, far_mate)]
    for device in greeted:
        pl.semaphore_signal(barrier, inc=1, device_id=device, device_id_type=MESH)
    pl.semaphore_wait(barrier, len(greeted))

    far, near = n // 2, n - 1 - n // 2
    streams = [
        (0, x_ref, xg, right, -1, far),
        (1, a_ref, ag, left, 1, far),
        (2, x_ref, xg, left, 1, near),
        (3, a_ref, ag, right, -1, near),
    ]

    def ring_copy(stream, step):
        index, own, gathered, target, sign, _ = stream
        block = part_at(place + sign * step, n)
        source = own.at[section] if step == 0 else gathered.at[block]
        return pltpu.make_async_remote_copy(
            src_ref=source, dst_ref=gathered.at[block],
            send_sem=ring_send.at[index, step], recv_sem=ring_recv.at[index, step],
            device_id=(section, target), device_id_type=MESH)

    rows = depth // W_PARTS
    pieces = [(slot, pl.ds(half * rows, rows)) for slot in range(slots) for half in range(W_PARTS)]

    def weight_copy(kind, number):
        slot, span = pieces[number]
        owner = chip_mate if kind == 2 else section
        mate = chip_mate if kind == 0 else core_mate
        source = wg.at[owner, slot, span] if kind == 2 else w_ref.at[0, slot, span]
        return pltpu.make_async_remote_copy(
            src_ref=source, dst_ref=wg.at[owner, slot, span],
            send_sem=w_send.at[kind, number], recv_sem=w_recv.at[kind, number],
            device_id=(mate, part), device_id_type=MESH)

    sends = []

    def go(copy):
        copy.start()
        sends.append(copy)

    for stream in streams:
        go(ring_copy(stream, 0))
    for number in range(len(pieces)):
        go(weight_copy(0, number))
        go(weight_copy(1, number))
    counts = []
    for number, mate in enumerate((core_mate, chip_mate, far_mate)):
        counts.append(pltpu.make_async_remote_copy(
            src_ref=c_ref, dst_ref=cg.at[section], send_sem=c_send.at[number],
            recv_sem=c_recv.at[number], device_id=(mate, part), device_id_type=MESH))
        go(counts[-1])
    own = pltpu.make_async_copy(c_ref, cg.at[section], own_sem)
    own.start()
    tiles_in.wait()

    local_rows = ag.shape[1]
    half = local_rows // 2
    lanes = lax.broadcasted_iota(jnp.int32, (local_rows, local_rows), 1) // half

    def spread(number, p):
        rows = pl.ds(pl.multiple_of(p * local_rows, local_rows), local_rows)
        dense[rows, rows] = ag[p, :, :local_rows]

        def put(j, block):
            q = lax.rem(p + 1 + j, n)
            columns = pl.ds(pl.multiple_of(q * local_rows, local_rows), local_rows)
            twice = jnp.concatenate([block, block], axis=1)
            dense[rows, columns] = jnp.where(lanes == bounds[section, q, p], twice, jnp.zeros_like(twice))

        def pair(c, carry):
            both = ag[p, :, pl.ds(pl.multiple_of((c + 1) * local_rows, local_rows), local_rows)]
            put(2 * c, both[:, :half])
            put(2 * c + 1, both[:, half:])
            return carry

        lax.fori_loop(0, (n - 1) // 2, pair, 0)
        put(n - 2, ag[p, :, (n // 2) * local_rows:])
        copy = pltpu.make_async_copy(dense.at[rows], dg.at[rows], d_sem.at[number])
        copy.start()
        return copy

    spreads = [spread(0, part)]

    for step in range(1, max(far, len(pieces)) + 1):
        for stream in streams:
            if step <= stream[5]:
                ring_copy(stream, step - 1).wait_recv()
                if step < stream[5]:
                    go(ring_copy(stream, step))
        if step <= len(pieces):
            weight_copy(0, step - 1).wait_recv()
            go(weight_copy(2, step - 1))
        for stream in (streams[1], streams[3]):
            if step <= stream[5]:
                spreads.append(spread(len(spreads), part_at(place + stream[4] * step, n)))
    for number in range(len(pieces)):
        weight_copy(1, number).wait_recv()
        weight_copy(2, number).wait_recv()
    for copy in counts:
        copy.wait_recv()
    for copy in sends:
        copy.wait_send()
    own.wait()
    for copy in spreads:
        copy.wait()


def layers_kernel(n, cg, x_ref, w_ref, xg, dg, wg, out, hidden, dense, weights, x_sem, d_sem, w_sem):
    section, part = lax.axis_index("section"), lax.axis_index("dom")
    local_rows, width = xg.shape[1], xg.shape[2]
    sections, slots = wg.shape[0], wg.shape[1]
    rows_all = n * local_rows

    def fetch(index, here, own, gathered, target, sem):
        @pl.when(index == here)
        def _():
            pltpu.make_async_copy(own, target, sem).start()

        @pl.when(index != here)
        def _():
            pltpu.make_async_copy(gathered.at[index], target, sem).start()

    def fetch_rows(p, carry):
        fetch(p, part, x_ref.at[section], xg, hidden.at[0, p], x_sem)
        return carry

    d_copy = pltpu.make_async_copy(dg, dense, d_sem)
    d_copy.start()
    lax.fori_loop(0, n, fetch_rows, 0)
    for s in range(sections):
        fetch(s, section, w_ref.at[0], wg, weights.at[s], w_sem.at[s])
    pltpu.make_async_copy(xg, hidden.at[0], x_sem).wait()
    d_copy.wait()

    def layer_rows(start, rows, now, later, s, k):
        span = pl.ds(pl.multiple_of(start, rows), rows)
        source = hidden.at[now].reshape(rows_all, width)
        aggregate = jnp.dot(dense[span, :], source[...], preferred_element_type=jnp.float32)
        mean_square = jnp.mean(aggregate * aggregate, axis=-1, keepdims=True)
        normed = (aggregate * lax.rsqrt(mean_square + 1e-06)).astype(jnp.bfloat16)
        projected = jnp.dot(normed, weights[s, k], preferred_element_type=jnp.float32)
        result = source[span, :].astype(jnp.float32) + jnp.maximum(projected, 0.0)
        hidden.at[later].reshape(rows_all, width)[span, :] = result.astype(jnp.bfloat16)

    chunk = min(1024, rows_all)
    counts = [cg[s, 0, 0] for s in range(sections)]
    total = sum(counts)
    done = jnp.int32(0)
    for s in range(sections):
        pltpu.make_async_copy(wg.at[s], weights.at[s], w_sem.at[s]).wait()
        for k in range(slots):
            number = done + k
            now = lax.rem(number, 2)
            active = k < counts[s]
            last = number == total - 1

            @pl.when(active & jnp.logical_not(last))
            def _():
                def body(c, carry):
                    layer_rows(c * chunk, chunk, now, 1 - now, s, k)
                    return carry
                lax.fori_loop(0, rows_all // chunk, body, 0)

            @pl.when(active & last)
            def _():
                layer_rows(part * local_rows, local_rows, now, 1 - now, s, k)

        done = done + counts[s]
        out[s] = hidden[lax.rem(done, 2), part]


def trade_kernel(o_ref, out, send, recv, own_sem):
    section, part = lax.axis_index("section"), lax.axis_index("dom")
    chip_mate, core_mate = flip(section, 1), flip(section, 0)
    mates = (flip(chip_mate, 0), chip_mate, core_mate)
    barrier = pltpu.get_barrier_semaphore()
    for mate in mates:
        pl.semaphore_signal(barrier, inc=1, device_id=(mate, part), device_id_type=MESH)
    own = pltpu.make_async_copy(o_ref.at[section], out.at[section], own_sem)
    own.start()
    pl.semaphore_wait(barrier, len(mates))
    copies = [
        pltpu.make_async_remote_copy(
            src_ref=o_ref.at[mate], dst_ref=out.at[section], send_sem=send.at[i],
            recv_sem=recv.at[i], device_id=(mate, part), device_id_type=MESH)
        for i, mate in enumerate(mates)
    ]
    for copy in copies:
        copy.start()
    for copy in copies:
        copy.wait()
    own.wait()


def local(features, adjacency, boundary, layer_counts, weights):
    n = lax.axis_size("dom")
    sections = lax.axis_size("section")
    micro, local_rows, width = features.shape
    slots = weights.shape[1]
    tile_width = adjacency.shape[3]
    tiles = adjacency.reshape(micro, local_rows, tile_width)
    counts = jnp.broadcast_to(layer_counts.reshape(1, 1), (8, 128))
    pieces = slots * W_PARTS
    bf16 = jnp.bfloat16
    dma = pltpu.SemaphoreType.DMA
    rows_all = n * local_rows
    xg, dg, wg, cg = pl.pallas_call(
        functools.partial(gather_kernel, n),
        out_shape=[
            jax.ShapeDtypeStruct((n, local_rows, width), bf16),
            jax.ShapeDtypeStruct((rows_all, rows_all), bf16),
            jax.ShapeDtypeStruct((sections,) + weights.shape[1:], bf16),
            jax.ShapeDtypeStruct((sections, 8, 128), jnp.int32),
        ],
        in_specs=[SMEM] + [ANY] * 4,
        out_specs=[ANY] * 4,
        scratch_shapes=[
            pltpu.VMEM((n, local_rows, tile_width), bf16),
            pltpu.VMEM((rows_all, rows_all), bf16),
            dma((n,)), dma,
            dma((4, n // 2)), dma((4, n // 2)), dma((3, pieces)), dma((3, pieces)),
            dma((3,)), dma((3,)), dma,
        ],
        compiler_params=pltpu.CompilerParams(
            collective_id=0, has_side_effects=True, vmem_limit_bytes=60 << 20),
        name="gather",
    )(boundary, features, tiles, weights, counts)

    mine = pl.pallas_call(
        functools.partial(layers_kernel, n),
        out_shape=jax.ShapeDtypeStruct((sections, local_rows, width), bf16),
        in_specs=[SMEM] + [ANY] * 5,
        out_specs=pl.BlockSpec(memory_space=pltpu.VMEM),
        scratch_shapes=[
            pltpu.VMEM((2, n, local_rows, width), bf16),
            pltpu.VMEM((rows_all, rows_all), bf16),
            pltpu.VMEM((sections,) + weights.shape[1:], bf16),
            dma, dma, dma((sections,)),
        ],
        compiler_params=pltpu.CompilerParams(vmem_limit_bytes=60 << 20),
        name="layers",
    )(cg, features, weights, xg, dg, wg)

    out = pl.pallas_call(
        trade_kernel,
        out_shape=jax.ShapeDtypeStruct((sections, local_rows, width), bf16),
        in_specs=[pl.BlockSpec(memory_space=pltpu.VMEM)],
        out_specs=pl.BlockSpec(memory_space=pltpu.VMEM),
        scratch_shapes=[dma((3,)), dma((3,)), dma],
        compiler_params=pltpu.CompilerParams(collective_id=1, has_side_effects=True),
        name="trade",
    )(mine)
    return out[None]


def solution(mesh):
    in_specs = (
        P(None, "dom", None),
        P(None, "dom", None, None),
        P(),
        P("section"),
        P("section", None, None, None),
    )
    out_specs = P("section", None, "dom", None)
    return jax.shard_map(local, mesh=mesh, in_specs=in_specs, out_specs=out_specs, check_vma=False)
```
